512 devices in a mesh: section: 8 (over y), row: 8 (over x, core), col: 8 (over z).
Axes of the slice: x: 4, y: 8, z: 8, core: 2. Of those that a mesh axis runs over, the one named last changes fastest.
Arguments:
- features: bfloat16 [12, 32, 96, 1024], P(None, 'row', None, 'col'), may hold values from -6 to 6
- conv_weight: bfloat16 [8, 3, 3, 3, 96, 96], P('section'), may hold values from -0.125 to 0.125
- norm_gain: float32 [8, 96], P('section'), may hold values from 0.1 to 1.9
- conv_bias: float32 [8, 96], P('section'), may hold values from -2 to 2
- cached: bfloat16 [8, 2, 32, 96, 1024], P('section', None, 'row', None, 'col'), may hold values from -4 to 4
Outputs:
- section_out: bfloat16 [8, 12, 32, 96, 1024], P('section', None, 'row', None, 'col')
The draws below stay inside these ranges and needn't reach their ends.
All inputs are finite; a program needn't handle non-finite values.
Results may differ from the reference program's by a relative error of at most 0.013.
Values may be sent and summed in bfloat16 or wider, within the bound.
No kernel may reach another device: no remote copies, remote signals or barrier semaphores. Data moves between devices by JAX's collectives and lax.ppermute only.
A program may use at most 64 MiB of HBM per device.

```python
import jax
import jax.numpy as jnp
from jax import lax

C = 96
GROUP_FR = 4
GROUPS = 3
LAYERS = 8
FRAMES = 12
HT = 32
WT = 1024
N_SECTION = 8


def shard_levels(own_key, dims, cuts, low, top_value):
    level, own = 1.0, jax.random.fold_in(own_key, 6)
    for axis_at, blocks in cuts:
        steps = jnp.exp(jax.random.uniform(jax.random.fold_in(own, axis_at), (blocks,), jnp.float32, low / len(cuts), top_value / len(cuts)))
        level = level * jnp.repeat(steps, dims[axis_at] // blocks).reshape([-1 if axis == axis_at else 1 for axis in range(len(dims))])
    return level


def noise(key, shape, deviation, reach, cuts=(), held_as=jnp.bfloat16):
    values = deviation * jax.random.normal(key, shape, jnp.float32)
    if cuts:
        values = values * shard_levels(key, shape, cuts, -0.22, 0.18)
    return jnp.clip(values, -reach, reach).astype(held_as)


def setup_inputs(seed: int = 0) -> dict:
    seeds = jax.random.split(jax.random.key(seed), 6)
    return {
        "features": noise(seeds[0], (FRAMES, HT, C, WT), 1.0, 6.0, ((1, 8), (3, 8))),
        "conv_weight": noise(seeds[1], (LAYERS, 3, 3, 3, C, C), (27 * C) ** -0.5, 0.125, ((0, 8),)),
        "norm_gain": jnp.clip(1.0 + 0.18 * jax.random.normal(seeds[2], (LAYERS, C), jnp.float32), 0.1, 1.9),
        "conv_bias": noise(seeds[3], (LAYERS, C), 0.3, 2.0, ((0, 8),), jnp.float32),
        "cached": noise(seeds[4], (LAYERS, 2, HT, C, WT), 0.5, 4.0, ((0, 8), (2, 8), (4, 8))),
    }


def prepare(inputs, gain):
    values = inputs.astype(jnp.float32)
    meansq = lax.optimization_barrier(jnp.mean(values * values, axis=2, keepdims=True))
    normed = values * lax.rsqrt(meansq + 1e-06) * gain[None, None, :, None]
    return jax.nn.silu(normed).astype(jnp.bfloat16)

def convolve(extended, kernel):
    padded = jnp.pad(extended, ((0, 0), (1, 1), (0, 0), (1, 1))).astype(jnp.float32)
    source = jnp.transpose(padded, (2, 0, 1, 3))[None]
    filters = jnp.transpose(kernel.astype(jnp.float32), (4, 3, 0, 1, 2))
    result = lax.conv_general_dilated(source, filters, (1, 1, 1), 'VALID', dimension_numbers=('NCDHW', 'OIDHW', 'NCDHW'), precision=lax.Precision.HIGHEST)
    return jnp.transpose(result[0], (1, 2, 0, 3))

def reference(features, conv_weight, norm_gain, conv_bias, cached):
    current = features
    results = []
    for block in range(N_SECTION):
        stored = cached[block]
        pieces = []
        for index in range(GROUPS):
            inputs = current[index * GROUP_FR:(index + 1) * GROUP_FR]
            normed = prepare(inputs, norm_gain[block])
            extended = jnp.concatenate([stored, normed], axis=0)
            stored = normed[-2:]
            conv = convolve(extended, conv_weight[block])
            output = inputs.astype(jnp.float32) + conv + conv_bias[block][None, None, :, None]
            pieces.append(output.astype(jnp.bfloat16))
        current = jnp.concatenate(pieces, axis=0)
        results.append(current)
    return jnp.stack(results)
```

```python
import jax
import jax.numpy as jnp
from jax import lax
from jax.experimental import pallas as pl
from jax.experimental.pallas import tpu as pltpu
from jax.sharding import PartitionSpec as P

C = 96
LAYERS = 8
FRAMES = 12
ROWS = 4
COLS = 128
OWN = 16
HALO = 8
WIN = OWN + 2 * HALO
LANES = 640
TAPS = 9 * C
WIDE = 896
VMEM = pl.BlockSpec(memory_space=pltpu.VMEM)
SMEM = pl.BlockSpec(memory_space=pltpu.SMEM)
F32 = jnp.float32
BF16 = jnp.bfloat16


def lanes_of(layer):
    used = (20 - 2 * layer) * WIN
    made = (18 - 2 * layer) * WIN
    return -(-used // 128) * 128, -(-made // 128) * 128


def shifted(block, offset):
    size = block.shape[-1]
    offset %= size
    return pltpu.roll(block, size - offset, 1) if offset else block


def edges_kernel(features, cached, right, left):
    lane = lax.broadcasted_iota(jnp.int32, (C, 128), 1)
    for group in range(4):
        ends = jnp.zeros((C, 128), F32)
        heads = jnp.zeros((C, 128), F32)
        for inner in range(4):
            frame = group * 4 + inner
            if frame >= FRAMES + 2:
                continue
            for row in range(ROWS):
                tile = (features[frame, row] if frame < FRAMES else cached[frame - FRAMES, row]).astype(F32)
                at = inner * 32 + row * 8
                here = jnp.logical_and(lane >= at, lane < at + 8)
                ends = jnp.where(here, shifted(tile, 120 - at), ends)
                heads = jnp.where(here, shifted(tile, -at), heads)
        right[group] = ends.astype(BF16)
        left[group] = heads.astype(BF16)


def windows_kernel(place, features, cached, before, after, own, spread):
    lane = lax.broadcasted_iota(jnp.int32, (C, 128), 1)
    section = place[0]

    def edge(block, frame, row, column):
        group, inner = divmod(frame, 4)
        at = inner * 32 + row * 8
        return shifted(block[group].astype(F32), at - row * WIN - column)

    def within(row, low, high):
        return jnp.logical_and(lane >= row * WIN + low, lane < row * WIN + high)

    for frame in range(FRAMES):
        total = jnp.zeros((C, 128), F32)
        for row in range(ROWS):
            tile = features[frame, row].astype(F32)
            amount = lax.rem(row * WIN + HALO - OWN * section + 256, 128)
            window = pltpu.roll(tile, amount, 1)
            first = jnp.logical_and(within(row, 0, HALO), section == 0)
            last = jnp.logical_and(within(row, WIN - HALO, WIN), section == LAYERS - 1)
            window = jnp.where(first, edge(before, frame, row, 0), window)
            window = jnp.where(last, edge(after, frame, row, WIN - HALO), window)
            total = jnp.where(within(row, 0, WIN), window, total)
        own[frame] = total.astype(BF16)
    for frame in range(2):
        for target in range(LAYERS):
            total = jnp.zeros((C, 128), F32)
            for row in range(ROWS):
                tile = cached[frame, row].astype(F32)
                window = shifted(tile, OWN * target - HALO - row * WIN)
                if target == 0:
                    window = jnp.where(within(row, 0, HALO), edge(before, FRAMES + frame, row, 0), window)
                if target == LAYERS - 1:
                    window = jnp.where(
                        within(row, WIN - HALO, WIN), edge(after, FRAMES + frame, row, WIN - HALO), window
                    )
                total = jnp.where(within(row, 0, WIN), window, total)
            spread[target, frame] = total.astype(BF16)


def blocks_kernel(f0, f1, f2, f3, f4, c0, c1, c2, c3, c4, weight, inside, out, act, taps, sums, here, ahead, held):
    for at, part in enumerate((f0, f1, f2, f3, f4)):
        act[:, :, at * 128 : (at + 1) * 128] = part[...]
    middle = lax.broadcasted_iota(jnp.int32, (C, 128), 1) % WIN
    middle = jnp.logical_and(middle >= HALO, middle < HALO + OWN)

    def spread_taps(values, start, base, count):
        for tap_row in range(3):
            for tap_col in range(3):
                block = shifted(values, base + tap_row * WIN + tap_col - 1)[:, :count]
                tap = tap_row * 3 + tap_col
                taps[tap * C : (tap + 1) * C, pl.ds(start, count)] = block.astype(BF16)

    for layer in range(LAYERS):
        used, made = lanes_of(layer)
        batch = {640: 3, 512: 4, 384: 4, 256: 6, 128: 12}[made]

        def column(at):
            parts = [weight[layer, 0:C, at + i : at + i + 1].astype(F32) for i in range(3)]
            return parts[0] + parts[1] + parts[2]

        gain = column(TAPS)
        bias = column(TAPS + 3)
        valid = inside[layer, :, 0:used]

        for frame in range(2):
            stored = jnp.concatenate([c[layer, frame] for c in (c0, c1, c2, c3, c4)], axis=1)
            spread_taps(stored.astype(F32), frame * made, layer * WIN, made)
        sums[0 : 2 * C, 0 : 2 * made] = jnp.dot(
            weight[layer, 0 : 2 * C, 0:TAPS], taps[:, 0 : 2 * made], preferred_element_type=F32
        )
        here[:, 0:made] = sums[0:C, 0:made] + sums[C : 2 * C, made : 2 * made] + bias
        ahead[:, 0:made] = sums[0:C, made : 2 * made] + bias

        def run(step, _, used=used, made=made, batch=batch, gain=gain, bias=bias, valid=valid, layer=layer):
            def prepare(inner, _):
                values = act[step * batch + inner, :, 0:used].astype(F32)
                meansq = jnp.sum(values * values, axis=0, keepdims=True) * (1.0 / C)
                scale = lax.rsqrt(meansq + 1e-06) * valid
                normed = values * scale * gain
                normed = (0.5 * normed) * (1.0 + jnp.tanh(0.5 * normed))
                spread_taps(normed, pl.multiple_of(inner * made, 128), 0, made)
                return 0

            lax.fori_loop(0, batch, prepare, 0)
            sums[:, 0 : batch * made] = jnp.dot(
                weight[layer, :, 0:TAPS], taps[:, 0 : batch * made], preferred_element_type=F32
            )

            def finish(inner, _):
                frame = step * batch + inner
                span = pl.ds(pl.multiple_of(inner * made, 128), made)
                inputs = shifted(act[frame, :, 0:used].astype(F32), WIN)[:, 0:made]
                total = inputs + here[:, 0:made] + sums[2 * C : 3 * C, span]
                here[:, 0:made] = ahead[:, 0:made] + sums[C : 2 * C, span]
                ahead[:, 0:made] = sums[0:C, span] + bias
                act[frame, :, 0:made] = total.astype(BF16)
                center = shifted(total, (7 - layer) * WIN)[:, 0:128]
                odd = lax.rem(frame, 2) == 1

                @pl.when(odd)
                def _():
                    both = jnp.where(middle, held[...], pltpu.roll(center, OWN, 1))
                    out[layer, frame // 2] = both.astype(BF16)

                @pl.when(jnp.logical_not(odd))
                def _():
                    held[...] = center

                return 0

            lax.fori_loop(0, batch, finish, 0)
            return 0

        lax.fori_loop(0, FRAMES // batch, run, 0)


def join_kernel(parts, out):
    lane = lax.broadcasted_iota(jnp.int32, (C, 128), 1)
    for frame in range(FRAMES):
        for row in range(ROWS):
            at = row * WIN + HALO + (OWN if frame % 2 else 0)
            total = jnp.zeros((C, 128), F32)
            for source in range(LAYERS):
                block = shifted(parts[source, frame // 2].astype(F32), at - source * OWN)
                mine = jnp.logical_and(lane >= source * OWN, lane < (source + 1) * OWN)
                total = jnp.where(mine, block, total)
            out[frame, row] = total.astype(BF16)


def call(kernel, shapes, scratch=(), limit=56, flops=0, moved=0, name=None):
    return pl.pallas_call(
        kernel,
        out_shape=[jax.ShapeDtypeStruct(s, BF16) for s in shapes],
        out_specs=[VMEM] * len(shapes),
        scratch_shapes=list(scratch),
        compiler_params=pltpu.CompilerParams(vmem_limit_bytes=limit << 20),
        cost_estimate=pl.CostEstimate(flops=flops, bytes_accessed=moved, transcendentals=0),
        name=name,
    )


def along(block, axis, distance):
    count = lax.axis_size(axis)
    route = [(i, i + distance) for i in range(count) if 0 <= i + distance < count]
    return lax.ppermute(block, axis, route)


def three_parts(values):
    high = values.astype(BF16)
    rest = values - high.astype(F32)
    mid = rest.astype(BF16)
    low = (rest - mid.astype(F32)).astype(BF16)
    return [high, mid, low]


def body(features, conv_weight, norm_gain, conv_bias, cached):
    section = lax.axis_index("section")
    row = lax.axis_index("row")
    col = lax.axis_index("col")
    cached = cached[0]

    matrix = jnp.transpose(conv_weight[0], (0, 4, 1, 2, 3)).reshape(3 * C, TAPS)
    extra = jnp.stack(three_parts(norm_gain[0]) + three_parts(conv_bias[0]), axis=1)
    extra = jnp.pad(extra, ((0, 2 * C), (0, WIDE - TAPS - 6)))
    matrix = jnp.concatenate([matrix, extra], axis=1)
    weights = lax.all_gather(matrix, "section")

    right, left = call(edges_kernel, [(4, C, 128)] * 2, name="edges")(features, cached)
    before = along(right, "col", 1)
    after = along(left, "col", -1)
    place = jnp.reshape(section, (1,)).astype(jnp.int32)
    own, spread = pl.pallas_call(
        windows_kernel,
        in_specs=[SMEM] + [VMEM] * 4,
        out_shape=[
            jax.ShapeDtypeStruct((FRAMES, C, 128), BF16),
            jax.ShapeDtypeStruct((LAYERS, 2, C, 128), BF16),
        ],
        out_specs=[VMEM] * 2,
        compiler_params=pltpu.CompilerParams(vmem_limit_bytes=32 << 20),
        name="windows",
    )(place, features, cached, before, after)
    stored = lax.all_to_all(spread, "section", 0, 0, tiled=True)
    steps = (2, 1, -1, -2)
    f = [along(own, "row", d) for d in steps]
    c = [along(stored, "row", d) for d in steps]
    f = [f[0], f[1], own, f[2], f[3]]
    c = [c[0], c[1], stored, c[2], c[3]]

    cell = jnp.arange(LANES, dtype=jnp.int32)[None, None, :]
    first = jnp.arange(LAYERS, dtype=jnp.int32)[:, None, None]
    at_row = row * ROWS - HALO + first + cell // WIN
    at_col = col * COLS + section * OWN - HALO + cell % WIN
    high = lax.axis_size("row") * ROWS
    wide = lax.axis_size("col") * COLS
    inside = (at_row >= 0) & (at_row < high) & (at_col >= 0) & (at_col < wide)
    inside = inside.astype(F32)

    (packed,) = call(
        blocks_kernel,
        [(LAYERS, FRAMES // 2, C, 128)],
        [
            pltpu.VMEM((FRAMES, C, LANES), BF16),
            pltpu.VMEM((TAPS, 2048), BF16),
            pltpu.VMEM((3 * C, 2048), F32),
            pltpu.VMEM((C, LANES), F32),
            pltpu.VMEM((C, LANES), F32),
            pltpu.VMEM((C, 128), F32),
        ],
        flops=18_000_000_000,
        moved=8_000_000,
        name="blocks",
    )(*f, *c, weights, inside)
    parts = lax.all_to_all(packed, "section", 0, 0, tiled=True)
    (joined,) = call(join_kernel, [(FRAMES, ROWS, C, COLS)], name="join")(parts)
    return joined[None]


def solution(mesh):
    return jax.shard_map(
        body,
        mesh=mesh,
        in_specs=(
            P(None, "row", None, "col"),
            P("section", None, None, None, None, None),
            P("section", None),
            P("section", None),
            P("section", None, "row", None, "col"),
        ),
        out_specs=P("section", None, "row", None, "col"),
        check_vma=False,
    )
```

```python
import jax
import jax.numpy as jnp
from jax import lax
from jax.experimental import pallas as pl
from jax.experimental.pallas import tpu as pltpu
from jax.sharding import PartitionSpec as P

C = 96
LAYERS = 8
FRAMES = 12
ROWS = 4
COLS = 128
OWN = 16
HALO = 8
WIN = OWN + 2 * HALO
GROUPS = 3
GROUP = 4
HIGH = ROWS + 2 * HALO
TAPS = 9 * C
WIDE = 896
VMEM = pl.BlockSpec(memory_space=pltpu.VMEM)
SMEM = pl.BlockSpec(memory_space=pltpu.SMEM)
F32 = jnp.float32
BF16 = jnp.bfloat16


def shifted(block, offset):
    size = block.shape[-1]
    offset %= size
    return pltpu.roll(block, size - offset, 1) if offset else block


def weights_kernel(place, taps, gain, bias, out, whole):
    for time in range(3):
        whole[time * C : (time + 1) * C, 0:TAPS] = taps[time].T
    values = jnp.concatenate([gain[...], bias[...], jnp.zeros((6, C), F32)], axis=0).T
    high = values.astype(BF16)
    rest = values - high.astype(F32)
    mid = rest.astype(BF16)
    low = (rest - mid.astype(F32)).astype(BF16)
    whole[0:C, TAPS:WIDE] = jnp.concatenate([high, mid, low, jnp.zeros((C, 8), BF16)], axis=1)
    whole[C : 3 * C, TAPS:WIDE] = jnp.zeros((2 * C, WIDE - TAPS), BF16)
    out[...] = whole[pl.ds(pl.multiple_of(place[1] * HALF, 16), HALF), :]


def windows_kernel(place, features, cached, own, spread):
    lane = lax.broadcasted_iota(jnp.int32, (C, 128), 1)
    section = place[0]

    def joined(pieces):
        total = pieces[0]
        for slot in (1, 2, 3):
            total = jnp.where(lane >= slot * WIN, pieces[slot], total)
        return total

    for group in range(GROUPS):
        for row in range(ROWS):
            pieces = []
            for slot in range(GROUP):
                amount = lax.rem(slot * WIN + HALO - OWN * section + 256, 128)
                pieces.append(pltpu.roll(features[group * GROUP + slot, row], amount, 1))
            own[group, row] = joined(pieces)
    for target in range(LAYERS):
        for pair in range(ROWS // 2):
            pieces = []
            for slot in range(4):
                tile = cached[slot % 2, 2 * pair + slot // 2]
                pieces.append(shifted(tile, OWN * target - HALO - slot * WIN))
            spread[target, pair] = joined(pieces)


STARTS = [sum(HIGH - 2 * i - 2 for i in range(layer)) for layer in range(LAYERS + 1)]
HALF = 3 * C // 2


def blocks_kernel(
    f0, f1, f2, f3, f4, c0, c1, c2, c3, c4, inside, gathered,
    out, act, taps0, taps1, taps2, sums0, sums1, sums2, early, gains, biases, weight, spare0, spare1, arrived,
):
    taps, sums, spare = (taps0, taps1, taps2), (sums0, sums1, sums2), (spare0, spare1)
    lane = lax.broadcasted_iota(jnp.int32, (C, 128), 1)
    middle = jnp.logical_and(lane % WIN >= HALO, lane % WIN < HALO + OWN)

    def tile(row):
        return pl.ds(row * 128 if isinstance(row, int) else pl.multiple_of(row * 128, 128), 128)

    def put(target, row, values):
        target[0:C, tile(row)] = pltpu.roll(values, 1, 1)
        target[C : 2 * C, tile(row)] = values
        target[2 * C : 3 * C, tile(row)] = pltpu.roll(values, 127, 1)

    def prepare(layer, group, row, stored):
        values = stored.astype(F32)
        meansq = jnp.sum(values * values, axis=0, keepdims=True) * (1.0 / C)
        scale = lax.rsqrt(meansq + 1e-06) * inside[row]
        half = values * scale * gains[layer]
        put(taps[group], row, (half * (1.0 + jnp.tanh(half))).astype(BF16))

    def multiply(layer, source, row, count, height, target, column):
        parts = [source[:, pl.ds((row + b) * 128, count * 128)] for b in range(3)]
        target[0:height, pl.ds(column * 128, count * 128)] = jnp.dot(
            weight[layer, 0:height, 0:TAPS], jnp.concatenate(parts, axis=0), preferred_element_type=F32
        )

    def finish(layer, group, row):
        now = tile(row - (layer + 1))
        cur = sums[group]
        if group:
            old, before = sums[group - 1], now
        else:
            old, before = early, tile(row - (layer + 1) + STARTS[layer])
        one = jnp.where(lane >= 3 * WIN, old[C : 2 * C, before], cur[C : 2 * C, now])
        two = jnp.where(lane >= 2 * WIN, old[0:C, before], cur[0:C, now])
        total = act[group, row].astype(F32) + biases[layer] + cur[2 * C : 3 * C, now]
        total = total + pltpu.roll(one, WIN, 1) + pltpu.roll(two, 2 * WIN, 1)
        stored = total.astype(BF16)
        act[group, row] = stored
        if layer + 1 < LAYERS:
            prepare(layer + 1, group, row, stored)

    def emit(layer, group):
        for pair in range(ROWS // 2):
            even = act[group, HALO + 2 * pair]
            odd = pltpu.roll(act[group, HALO + 2 * pair + 1], OWN, 1)
            out[layer, group * 2 + pair] = jnp.where(middle, even, odd)

    def loop(count, step, unroll=1):
        def run(index, _):
            step(index)
            return 0

        lax.fori_loop(0, count, run, 0, unroll=unroll)

    copies = [
        pltpu.make_async_copy(gathered.at[layer], weight.at[layer], arrived.at[layer]) for layer in range(LAYERS)
    ]
    for copy in copies:
        copy.start()
    for at, part in enumerate((f0, f1, f2, f3, f4)):
        act[:, at * ROWS : (at + 1) * ROWS] = part[...]
    for layer in range(LAYERS):
        copies[layer].wait()

        def column(at, layer=layer):
            parts = [weight[layer, 0:C, at + 8 * i : at + 8 * i + 1].astype(F32) for i in range(3)]
            return jnp.broadcast_to(parts[0] + parts[1] + parts[2], (C, 128))

        gains[layer] = 0.5 * column(TAPS)
        biases[layer] = column(TAPS + 1)
        if layer == 0:
            for group in range(GROUPS):
                loop(HIGH, lambda row, group=group: prepare(0, group, row, act[group, row]), 4)

    for layer in range(LAYERS):
        source = spare[layer % 2]
        for row in range(layer, HIGH - layer):
            stored = (c0, c1, c2, c3, c4)[row // ROWS][layer, row % ROWS // 2]
            put(source, row, stored if row % 2 else pltpu.roll(stored, 64, 1))
        multiply(layer, source, layer, HIGH - 2 * layer - 2, 2 * C, early, STARTS[layer])

    behind = None
    for layer in range(LAYERS):
        rows = HIGH - 2 * layer - 2
        for group in range(GROUPS):

            multiply(layer, taps[group], layer, rows, 3 * C, sums[group], 0)
            if behind is not None:
                for row in range(behind[0] + 1, HIGH - behind[0] - 1):
                    finish(*behind, row)
                emit(*behind)
            behind = (layer, group)
    loop(ROWS, lambda index: finish(*behind, LAYERS + index))
    emit(*behind)


def join_kernel(parts, out):
    lane = lax.broadcasted_iota(jnp.int32, (C, 128), 1)
    for at in range(FRAMES // 2):
        tiles = [shifted(parts[source, at], HALO) for source in range(LAYERS)]
        for bit in (1, 2, 4):
            low = (lane // OWN) % (2 * bit) < bit
            for first in range(LAYERS):
                if first & bit:
                    continue
                one, two = tiles[first], tiles[first + bit]
                tiles[first] = jnp.where(low, one, shifted(two, -OWN * bit))
                tiles[first + bit] = jnp.where(low, shifted(one, OWN * bit), two)
        for k in range(LAYERS):
            out[at // 2 * GROUP + k // 2, at % 2 * 2 + k % 2] = tiles[k]


def along(block, axes, distance):
    count = lax.axis_size(axes)
    route = [(i, i + distance) for i in range(count) if 0 <= i + distance < count]
    return lax.ppermute(block, axes, route)


def mended(block):
    sections, cols = lax.axis_size("section"), lax.axis_size("col")
    last = (sections - 1) * cols
    route = [(i, i + 1) for i in range(cols - 1)] + [(last + i + 1, last + i) for i in range(cols - 1)]
    beyond = lax.ppermute(block, ("section", "col"), route)
    section = lax.axis_index("section")
    column = jnp.arange(128, dtype=jnp.int32) % WIN
    ends = (section == 0) & (column < HALO) | (section == sections - 1) & (column >= WIN - HALO)
    return jnp.where(ends, beyond, block)


def vmem(size):
    return pltpu.CompilerParams(vmem_limit_bytes=size << 20)


def body(features, conv_weight, norm_gain, conv_bias, cached):
    section = lax.axis_index("section")
    row = lax.axis_index(("x", "core"))
    col = lax.axis_index("col")
    place = jnp.stack([section, lax.axis_index("core")]).astype(jnp.int32)

    mine = pl.pallas_call(
        weights_kernel,
        in_specs=[SMEM] + [VMEM] * 3,
        out_shape=jax.ShapeDtypeStruct((HALF, WIDE), BF16),
        out_specs=VMEM,
        scratch_shapes=[pltpu.VMEM((3 * C, WIDE), BF16)],
        compiler_params=vmem(32),
        name="weights",
    )(place, conv_weight.reshape(3, TAPS, C), norm_gain, conv_bias)
    gathered = lax.all_gather(mine, ("section", "core")).reshape(LAYERS, 3 * C, WIDE)

    own, spread = pl.pallas_call(
        windows_kernel,
        in_specs=[SMEM] + [VMEM] * 2,
        out_shape=[
            jax.ShapeDtypeStruct((GROUPS, ROWS, C, 128), BF16),
            jax.ShapeDtypeStruct((LAYERS, 2, C, 128), BF16),
        ],
        out_specs=[VMEM] * 2,
        compiler_params=vmem(32),
        name="windows",
    )(place, features, cached[0])
    stored = mended(lax.all_to_all(spread, "section", 0, 0, tiled=True))
    own = mended(own)
    steps = (2, 1, -1, -2)
    f = [along(own, ("x", "core"), d) for d in steps]
    c = [along(stored[0 : LAYERS // 2] if abs(d) == 2 else stored, ("x", "core"), d) for d in steps]
    f = [f[0], f[1], own, f[2], f[3]]
    c = [c[0], c[1], stored, c[2], c[3]]

    at_row = row * ROWS - HALO + jnp.arange(HIGH, dtype=jnp.int32)[:, None, None]
    at_col = col * COLS + section * OWN - HALO + jnp.arange(128, dtype=jnp.int32)[None, None, :] % WIN
    high = lax.axis_size(("x", "core")) * ROWS
    wide = lax.axis_size("col") * COLS
    inside = (at_row >= 0) & (at_row < high) & (at_col >= 0) & (at_col < wide)
    inside = inside.astype(F32)

    packed = pl.pallas_call(
        blocks_kernel,
        in_specs=[VMEM] * 11 + [pl.BlockSpec(memory_space=pl.ANY)],
        out_shape=jax.ShapeDtypeStruct((LAYERS, FRAMES // 2, C, 128), BF16),
        out_specs=VMEM,
        scratch_shapes=[
            pltpu.VMEM((GROUPS, HIGH, C, 128), BF16),
            *[pltpu.VMEM((3 * C, HIGH * 128), BF16)] * GROUPS,
            *[pltpu.VMEM((3 * C, (HIGH - 2) * 128), F32)] * GROUPS,
            pltpu.VMEM((2 * C, STARTS[LAYERS] * 128), F32),
            pltpu.VMEM((LAYERS, C, 128), F32),
            pltpu.VMEM((LAYERS, C, 128), F32),
            pltpu.VMEM((LAYERS, 3 * C, WIDE), BF16),
            *[pltpu.VMEM((3 * C, HIGH * 128), BF16)] * 2,
            pltpu.SemaphoreType.DMA((LAYERS,)),
        ],
        compiler_params=vmem(56),
        cost_estimate=pl.CostEstimate(flops=18_000_000_000, bytes_accessed=8_000_000, transcendentals=0),
        name="blocks",
    )(*f, *c, inside, gathered)
    parts = lax.all_to_all(packed, "section", 0, 0, tiled=True)
    joined = pl.pallas_call(
        join_kernel,
        in_specs=[VMEM],
        out_shape=jax.ShapeDtypeStruct((FRAMES, ROWS, C, COLS), BF16),
        out_specs=VMEM,
        compiler_params=vmem(32),
        name="join",
    )(parts)
    return joined[None]


def solution(mesh):
    sections, rows, cols = (mesh.shape[name] for name in ("section", "row", "col"))
    cores = jax.sharding.Mesh(mesh.devices.reshape(sections, rows // 2, 2, cols), ("section", "x", "core", "col"))
    return jax.shard_map(
        body,
        mesh=cores,
        in_specs=(
            P(None, ("x", "core"), None, "col"),
            P("section", None, None, None, None, None),
            P("section", None),
            P("section", None),
            P("section", None, ("x", "core"), None, "col"),
        ),
        out_specs=P("section", None, ("x", "core"), None, "col"),
        check_vma=False,
    )
```

```python
import jax
import jax.numpy as jnp
from jax import lax
from jax.experimental import pallas as pl
from jax.experimental.pallas import tpu as pltpu
from jax.sharding import PartitionSpec as P

C = 96
LAYERS = 8
FRAMES = 12
ROWS = 4
COLS = 128
OWN = 16
HALO = 8
WIN = OWN + 2 * HALO
GROUPS = 3
GROUP = 4
HIGH = ROWS + 2 * HALO
TAPS = 9 * C
WIDE = 896
VMEM = pl.BlockSpec(memory_space=pltpu.VMEM)
SMEM = pl.BlockSpec(memory_space=pltpu.SMEM)
F32 = jnp.float32
BF16 = jnp.bfloat16


def shifted(block, offset):
    size = block.shape[-1]
    offset %= size
    return pltpu.roll(block, size - offset, 1) if offset else block


def weights_kernel(place, taps_at, gain_at, bias_at, out, taps, gain, bias, whole, arrived):
    pairs = ((taps_at, taps), (gain_at, gain), (bias_at, bias))
    copies = [pltpu.make_async_copy(*pair, arrived.at[at]) for at, pair in enumerate(pairs)]
    for copy in copies:
        copy.start()
    for copy in copies:
        copy.wait()
    for time in range(3):
        whole[time * C : (time + 1) * C, 0:TAPS] = taps[time].T
    values = jnp.concatenate([gain[...], bias[...], jnp.zeros((6, C), F32)], axis=0).T
    high = values.astype(BF16)
    rest = values - high.astype(F32)
    mid = rest.astype(BF16)
    low = (rest - mid.astype(F32)).astype(BF16)
    whole[0:C, TAPS:WIDE] = jnp.concatenate([high, mid, low, jnp.zeros((C, 8), BF16)], axis=1)
    whole[C : 3 * C, TAPS:WIDE] = jnp.zeros((2 * C, WIDE - TAPS), BF16)
    out[...] = whole[pl.ds(pl.multiple_of(place[1] * HALF, 16), HALF), :]


def edges_kernel(features, cached, right, left):
    lane = lax.broadcasted_iota(jnp.int32, (C, 128), 1)
    for group in range(4):
        ends = heads = jnp.zeros((C, 128), BF16)
        for inner in range(4):
            frame = group * 4 + inner
            if frame >= FRAMES + 2:
                continue
            for row in range(ROWS):
                tile = features[frame, row] if frame < FRAMES else cached[frame - FRAMES, row]
                at = inner * 32 + row * HALO
                here = jnp.logical_and(lane >= at, lane < at + HALO)
                ends = jnp.where(here, shifted(tile, 120 - at), ends)
                heads = jnp.where(here, shifted(tile, -at), heads)
        right[group] = ends
        left[group] = heads


def windows_kernel(place, features, cached, before, after, own, spread):
    lane = lax.broadcasted_iota(jnp.int32, (C, 128), 1)
    section = place[0]

    def edge(block, frame, row, slot, column):
        at = frame % 4 * 32 + row * HALO
        return shifted(block[frame // 4], at - slot * WIN - column)

    def joined(pieces):
        total = pieces[0]
        for slot in (1, 2, 3):
            total = jnp.where(lane >= slot * WIN, pieces[slot], total)
        return total

    def mended(total, block, cells, column):
        for slot, (frame, row) in enumerate(cells):
            at = slot * WIN + column
            here = jnp.logical_and(lane >= at, lane < at + HALO)
            total = jnp.where(here, edge(block, frame, row, slot, column), total)
        return total

    for target in range(LAYERS):
        for pair in range(ROWS // 2):
            cells = [(slot % 2, 2 * pair + slot // 2) for slot in range(4)]
            pieces = [
                shifted(cached[frame, row], OWN * target - HALO - slot * WIN)
                for slot, (frame, row) in enumerate(cells)
            ]
            total = joined(pieces)
            cells = [(FRAMES + frame, row) for frame, row in cells]
            if target == 0:
                total = mended(total, before, cells, 0)
            if target == LAYERS - 1:
                total = mended(total, after, cells, WIN - HALO)
            spread[target, pair] = total
    for group in range(GROUPS):
        for row in range(ROWS):
            pieces = []
            for slot in range(GROUP):
                amount = lax.rem(slot * WIN + HALO - OWN * section + 256, 128)
                pieces.append(pltpu.roll(features[group * GROUP + slot, row], amount, 1))
            own[group, row] = joined(pieces)

    @pl.when(section == 0)
    def _():
        for group in range(GROUPS):
            for row in range(ROWS):
                cells = [(group * GROUP + slot, row) for slot in range(GROUP)]
                own[group, row] = mended(own[group, row], before, cells, 0)

    @pl.when(section == LAYERS - 1)
    def _():
        for group in range(GROUPS):
            for row in range(ROWS):
                cells = [(group * GROUP + slot, row) for slot in range(GROUP)]
                own[group, row] = mended(own[group, row], after, cells, WIN - HALO)


ODD = HIGH // 2
STARTS = [sum(HIGH - 2 * i - 2 for i in range(layer)) for layer in range(LAYERS + 1)]
HALF = 3 * C // 2


def blocks_kernel(
    f0, f1, f2, f3, f4, c0, c1, c2, c3, c4, inside, gathered,
    out, act, taps0, taps1, taps2, sums0, sums1, sums2, early, gains, biases, weight, spare0, spare1, arrived,
):
    taps, sums, spare = (taps0, taps1, taps2), (sums0, sums1, sums2), (spare0, spare1)
    lane = lax.broadcasted_iota(jnp.int32, (C, 128), 1)
    middle = jnp.logical_and(lane % WIN >= HALO, lane % WIN < HALO + OWN)

    def tile(row):
        return pl.ds(row * 128 if isinstance(row, int) else pl.multiple_of(row * 128, 128), 128)

    def put(target, row, values):
        target[0:C, tile(row)] = pltpu.roll(values, 1, 1)
        target[C : 2 * C, tile(row)] = values
        target[2 * C : 3 * C, tile(row)] = pltpu.roll(values, 127, 1)

    def prepare(layer, group, row, stored):
        values = stored.astype(F32)
        meansq = jnp.sum(values * values, axis=0, keepdims=True) * (1.0 / C)
        scale = lax.rsqrt(meansq + 1e-06) * inside[row]
        half = values * scale * gains[layer]
        put(taps[group], row, (half * (1.0 + jnp.tanh(half))).astype(BF16))

    def multiply(layer, source, row, count, height, target, column):
        parts = [source[:, pl.ds((row + b) * 128, count * 128)] for b in range(3)]
        target[0:height, pl.ds(column * 128, count * 128)] = jnp.dot(
            weight[layer, 0:height, 0:TAPS], jnp.concatenate(parts, axis=0), preferred_element_type=F32
        )

    def finish(layer, group, row):
        now = tile(row - (layer + 1))
        cur = sums[group]
        if group:
            old_one, old_two = sums[group - 1][C : 2 * C, now], sums[group - 1][0:C, now]
        else:
            pair = tile((row - (layer + 1) + STARTS[layer]) // 2)
            old_one, old_two = early[C : 2 * C, pair], early[0:C, pair]
            if (row - layer) % 2:
                old_one, old_two = pltpu.roll(old_one, 64, 1), pltpu.roll(old_two, 64, 1)
        one = jnp.where(lane >= 3 * WIN, old_one, cur[C : 2 * C, now])
        two = jnp.where(lane >= 2 * WIN, old_two, cur[0:C, now])
        total = act[group, row].astype(F32) + biases[layer] + cur[2 * C : 3 * C, now]
        total = total + pltpu.roll(one, WIN, 1) + pltpu.roll(two, 2 * WIN, 1)
        stored = total.astype(BF16)
        act[group, row] = stored
        if layer + 1 < LAYERS:
            prepare(layer + 1, group, row, stored)

    def emit(layer, group):
        for pair in range(ROWS // 2):
            even = act[group, HALO + 2 * pair]
            odd = pltpu.roll(act[group, HALO + 2 * pair + 1], OWN, 1)
            out[layer, group * 2 + pair] = jnp.where(middle, even, odd)

    def loop(count, step, unroll=1):
        def run(index, _):
            step(index)
            return 0

        lax.fori_loop(0, count, run, 0, unroll=unroll)

    copies = [
        pltpu.make_async_copy(gathered.at[layer], weight.at[layer], arrived.at[layer]) for layer in range(LAYERS)
    ]
    for copy in copies:
        copy.start()
    for at, part in enumerate((f0, f1, f2, f3, f4)):
        act[:, at * ROWS : (at + 1) * ROWS] = part[...]
    for layer in range(LAYERS):
        copies[layer].wait()

        def column(at, layer=layer):
            parts = [weight[layer, 0:C, at + 8 * i : at + 8 * i + 1].astype(F32) for i in range(3)]
            return jnp.broadcast_to(parts[0] + parts[1] + parts[2], (C, 128))

        gains[layer] = 0.5 * column(TAPS)
        biases[layer] = column(TAPS + 1)
    def mixed(one, two):
        return pltpu.roll(jnp.where(lane >= 64, one, two), 64, 1)

    for layer in range(LAYERS):
        source, pairs = spare[layer % 2], HIGH // 2 - layer - 1
        for at in range(2 * pairs + 1):
            low = (layer + at) // 2
            stored = (c0, c1, c2, c3, c4)[low // 2][layer, low % 2]
            if (layer + at) % 2:
                stored = mixed(stored, (c0, c1, c2, c3, c4)[(low + 1) // 2][layer, (low + 1) % 2])
            put(source, at // 2 + at % 2 * ODD, stored)
        parts = [source[:, at * 128 : (at + pairs) * 128] for at in (0, ODD, 1)]
        early[:, STARTS[layer] * 64 : STARTS[layer + 1] * 64] = jnp.dot(
            weight[layer, 0 : 2 * C, 0:TAPS], jnp.concatenate(parts, axis=0), preferred_element_type=F32
        )
    for row in range(HIGH):
        prepare(0, 0, row, act[0, row])

    behind = None
    for layer in range(LAYERS):
        rows = HIGH - 2 * layer - 2
        for group in range(GROUPS):

            multiply(layer, taps[group], layer, rows, 3 * C, sums[group], 0)
            if layer == 0 and group + 1 < GROUPS:
                for row in range(HIGH):
                    prepare(0, group + 1, row, act[group + 1, row])
            if behind is not None:
                for row in range(behind[0] + 1, HIGH - behind[0] - 1):
                    finish(*behind, row)
                emit(*behind)
            behind = (layer, group)
    loop(ROWS, lambda index: finish(*behind, LAYERS + index))
    emit(*behind)


def join_kernel(parts, out):
    lane = lax.broadcasted_iota(jnp.int32, (C, 128), 1)
    for at in range(FRAMES // 2):
        tiles = [shifted(parts[source, at], HALO) for source in range(LAYERS)]
        for bit in (1, 2, 4):
            low = (lane // OWN) % (2 * bit) < bit
            for first in range(LAYERS):
                if first & bit:
                    continue
                one, two = tiles[first], tiles[first + bit]
                tiles[first] = jnp.where(low, one, shifted(two, -OWN * bit))
                tiles[first + bit] = jnp.where(low, shifted(one, OWN * bit), two)
        for k in range(LAYERS):
            out[at // 2 * GROUP + k // 2, at % 2 * 2 + k % 2] = tiles[k]


def along(block, axes, distance):
    count = lax.axis_size(axes)
    route = [(i, i + distance) for i in range(count) if 0 <= i + distance < count]
    return lax.ppermute(block, axes, route)


def vmem(size):
    return pltpu.CompilerParams(vmem_limit_bytes=size << 20)


def body(features, conv_weight, norm_gain, conv_bias, cached):
    section = lax.axis_index("section")
    row = lax.axis_index(("x", "core"))
    col = lax.axis_index("col")
    place = jnp.stack([section, lax.axis_index("core")]).astype(jnp.int32)

    mine = pl.pallas_call(
        weights_kernel,
        in_specs=[SMEM] + [pl.BlockSpec(memory_space=pltpu.HBM)] * 3,
        out_shape=jax.ShapeDtypeStruct((HALF, WIDE), BF16),
        out_specs=VMEM,
        scratch_shapes=[
            pltpu.VMEM((3, TAPS, C), BF16),
            pltpu.VMEM((1, C), F32),
            pltpu.VMEM((1, C), F32),
            pltpu.VMEM((3 * C, WIDE), BF16),
            pltpu.SemaphoreType.DMA((3,)),
        ],
        compiler_params=vmem(32),
        name="weights",
    )(place, conv_weight.reshape(3, TAPS, C), norm_gain, conv_bias)
    gathered = lax.all_gather(mine, ("section", "core")).reshape(LAYERS, 3 * C, WIDE)

    right, left = pl.pallas_call(
        edges_kernel,
        in_specs=[VMEM] * 2,
        out_shape=[jax.ShapeDtypeStruct((4, C, 128), BF16)] * 2,
        out_specs=[VMEM] * 2,
        compiler_params=vmem(32),
        name="edges",
    )(features, cached[0])
    before = along(right, "col", 1)
    after = along(left, "col", -1)
    own, spread = pl.pallas_call(
        windows_kernel,
        in_specs=[SMEM] + [VMEM] * 4,
        out_shape=[
            jax.ShapeDtypeStruct((GROUPS, ROWS, C, 128), BF16),
            jax.ShapeDtypeStruct((LAYERS, 2, C, 128), BF16),
        ],
        out_specs=[VMEM] * 2,
        compiler_params=vmem(32),
        name="windows",
    )(place, features, cached[0], before, after)
    stored = lax.all_to_all(spread, "section", 0, 0, tiled=True)
    steps = (1, -1, 2, -2)
    f = [along(own, ("x", "core"), d) for d in steps]
    stored, *f = lax.optimization_barrier((stored, *f))
    c = [along(stored[0 : LAYERS // 2] if abs(d) == 2 else stored, ("x", "core"), d) for d in steps]
    f = [f[2], f[0], own, f[1], f[3]]
    c = [c[2], c[0], stored, c[1], c[3]]

    at_row = row * ROWS - HALO + jnp.arange(HIGH, dtype=jnp.int32)[:, None, None]
    at_col = col * COLS + section * OWN - HALO + jnp.arange(128, dtype=jnp.int32)[None, None, :] % WIN
    high = lax.axis_size(("x", "core")) * ROWS
    wide = lax.axis_size("col") * COLS
    inside = (at_row >= 0) & (at_row < high) & (at_col >= 0) & (at_col < wide)
    inside = inside.astype(F32)

    packed = pl.pallas_call(
        blocks_kernel,
        in_specs=[VMEM] * 11 + [pl.BlockSpec(memory_space=pl.ANY)],
        out_shape=jax.ShapeDtypeStruct((LAYERS, FRAMES // 2, C, 128), BF16),
        out_specs=VMEM,
        scratch_shapes=[
            pltpu.VMEM((GROUPS, HIGH, C, 128), BF16),
            *[pltpu.VMEM((3 * C, HIGH * 128), BF16)] * GROUPS,
            *[pltpu.VMEM((3 * C, (HIGH - 2) * 128), F32)] * GROUPS,
            pltpu.VMEM((2 * C, STARTS[LAYERS] * 64), F32),
            pltpu.VMEM((LAYERS, C, 128), F32),
            pltpu.VMEM((LAYERS, C, 128), F32),
            pltpu.VMEM((LAYERS, 3 * C, WIDE), BF16),
            *[pltpu.VMEM((3 * C, HIGH * 128), BF16)] * 2,
            pltpu.SemaphoreType.DMA((LAYERS,)),
        ],
        compiler_params=vmem(56),
        cost_estimate=pl.CostEstimate(flops=18_000_000_000, bytes_accessed=8_000_000, transcendentals=0),
        name="blocks",
    )(*f, *c, inside, gathered)
    parts = lax.all_to_all(packed, "section", 0, 0, tiled=True)
    joined = pl.pallas_call(
        join_kernel,
        in_specs=[VMEM],
        out_shape=jax.ShapeDtypeStruct((FRAMES, ROWS, C, COLS), BF16),
        out_specs=VMEM,
        compiler_params=vmem(32),
        name="join",
    )(parts)
    return joined[None]


def solution(mesh):
    sections, rows, cols = (mesh.shape[name] for name in ("section", "row", "col"))
    cores = jax.sharding.Mesh(mesh.devices.reshape(sections, rows // 2, 2, cols), ("section", "x", "core", "col"))
    return jax.shard_map(
        body,
        mesh=cores,
        in_specs=(
            P(None, ("x", "core"), None, "col"),
            P("section", None, None, None, None, None),
            P("section", None),
            P("section", None),
            P("section", None, ("x", "core"), None, "col"),
        ),
        out_specs=P("section", None, ("x", "core"), None, "col"),
        check_vma=False,
    )
```

```python
import jax
import jax.numpy as jnp
from jax import lax
from jax.experimental import pallas as pl
from jax.experimental.pallas import tpu as pltpu
from jax.sharding import PartitionSpec as P

C = 96
LAYERS = 8
FRAMES = 12
ROWS = 4
COLS = 128
OWN = 16
HALO = 8
WIN = OWN + 2 * HALO
GROUPS = 3
GROUP = 4
HIGH = ROWS + 2 * HALO
TAPS = 9 * C
WIDE = 896
VMEM = pl.BlockSpec(memory_space=pltpu.VMEM)
SMEM = pl.BlockSpec(memory_space=pltpu.SMEM)
F32 = jnp.float32
BF16 = jnp.bfloat16


def shifted(block, offset):
    size = block.shape[-1]
    offset %= size
    return pltpu.roll(block, size - offset, 1) if offset else block


def weights_kernel(place, taps, small, out, whole):
    for time in range(3):
        whole[time * C : (time + 1) * C, 0:TAPS] = taps[time].T
    values = small[...].T
    high = values.astype(BF16)
    rest = values - high.astype(F32)
    mid = rest.astype(BF16)
    low = (rest - mid.astype(F32)).astype(BF16)
    whole[0:C, TAPS:WIDE] = jnp.concatenate([high, mid, low, jnp.zeros((C, 8), BF16)], axis=1)
    whole[C : 3 * C, TAPS:WIDE] = jnp.zeros((2 * C, WIDE - TAPS), BF16)
    out[...] = whole[pl.ds(pl.multiple_of(place[1] * HALF, 16), HALF), :]


def gathered_ends(tiles, column):
    lane = lax.broadcasted_iota(jnp.int32, (C, 128), 1)
    total = shifted(tiles[0], column)
    for at in (1, 2, 3):
        total = jnp.where(lane % WIN >= at * HALO, shifted(tiles[at], column - at * HALO), total)
    return total


def windows_kernel(place, features, cached, own, spread, ends):
    lane = lax.broadcasted_iota(jnp.int32, (C, 128), 1)
    section = place[0]

    def joined(pieces):
        total = pieces[0]
        for slot in (1, 2, 3):
            total = jnp.where(lane >= slot * WIN, pieces[slot], total)
        return total

    for target in range(LAYERS):
        for pair in range(ROWS // 2):
            pieces = []
            for slot in range(4):
                tile = cached[slot % 2, 2 * pair + slot // 2]
                pieces.append(shifted(tile, OWN * target - HALO - slot * WIN))
            spread[target, pair] = joined(pieces)
    for group in range(GROUPS):
        for row in range(ROWS):
            pieces = []
            for slot in range(GROUP):
                amount = lax.rem(slot * WIN + HALO - OWN * section + 256, 128)
                pieces.append(pltpu.roll(features[group * GROUP + slot, row], amount, 1))
            own[group, row] = joined(pieces)

    @pl.when(section == 0)
    def _():
        for group in range(GROUPS):
            ends[group] = gathered_ends([own[group, row] for row in range(ROWS)], 0)

    @pl.when(section != 0)
    def _():
        for group in range(GROUPS):
            ends[group] = gathered_ends([own[group, row] for row in range(ROWS)], WIN - HALO)


def ends_kernel(place, block, ends):
    section = place[0]

    @pl.when(section == 0)
    def _():
        for at in range(4):
            ends[at] = gathered_ends([block[at * 4 + i] for i in range(4)], 0)

    @pl.when(section != 0)
    def _():
        for at in range(4):
            ends[at] = gathered_ends([block[at * 4 + i] for i in range(4)], WIN - HALO)


def mend_kernel(place, block, beyond, out, *first):
    lane = lax.broadcasted_iota(jnp.int32, (C, 128), 1) % WIN
    section = place[0]
    out[...] = block[...]

    @pl.when(section == 0)
    def _():
        for at in range(block.shape[0]):
            out[at] = jnp.where(lane < HALO, shifted(beyond[at // 4], at % 4 * HALO), block[at])

    @pl.when(section == LAYERS - 1)
    def _():
        for at in range(block.shape[0]):
            piece = shifted(beyond[at // 4], at % 4 * HALO - (WIN - HALO))
            out[at] = jnp.where(lane >= WIN - HALO, piece, block[at])

    for half in first:
        half[...] = out[0 : half.shape[0]]


ODD = HIGH // 2
STARTS = [sum(HIGH - 2 * i - 2 for i in range(layer)) for layer in range(LAYERS + 1)]
HALF = 3 * C // 2


def blocks_kernel(
    f0, f1, f2, f3, f4, c0, c1, c2, c3, c4, inside, gathered,
    out, act, taps0, taps1, taps2, sums0, sums1, sums2, early, gains, biases, weight, spare0, spare1, arrived,
):
    taps, sums, spare = (taps0, taps1, taps2), (sums0, sums1, sums2), (spare0, spare1)
    lane = lax.broadcasted_iota(jnp.int32, (C, 128), 1)
    middle = jnp.logical_and(lane % WIN >= HALO, lane % WIN < HALO + OWN)

    def tile(row):
        return pl.ds(row * 128 if isinstance(row, int) else pl.multiple_of(row * 128, 128), 128)

    def put(target, row, values):
        target[0:C, tile(row)] = pltpu.roll(values, 1, 1)
        target[C : 2 * C, tile(row)] = values
        target[2 * C : 3 * C, tile(row)] = pltpu.roll(values, 127, 1)

    def prepare(layer, group, row, stored):
        values = stored.astype(F32)
        meansq = jnp.sum(values * values, axis=0, keepdims=True) * (1.0 / C)
        scale = lax.rsqrt(meansq + 1e-06) * inside[row]
        half = values * scale * gains[layer]
        put(taps[group], row, (half * (1.0 + jnp.tanh(half))).astype(BF16))

    def multiply(layer, source, row, count, height, target, column):
        parts = [source[:, pl.ds((row + b) * 128, count * 128)] for b in range(3)]
        target[0:height, pl.ds(column * 128, count * 128)] = jnp.dot(
            weight[layer, 0:height, 0:TAPS], jnp.concatenate(parts, axis=0), preferred_element_type=F32
        )

    def finish(layer, group, row):
        now = tile(row - (layer + 1))
        cur = sums[group]
        if group:
            old_one, old_two = sums[group - 1][C : 2 * C, now], sums[group - 1][0:C, now]
        else:
            pair = tile((row - (layer + 1) + STARTS[layer]) // 2)
            old_one, old_two = early[C : 2 * C, pair], early[0:C, pair]
            if (row - layer) % 2:
                old_one, old_two = pltpu.roll(old_one, 64, 1), pltpu.roll(old_two, 64, 1)
        one = jnp.where(lane >= 3 * WIN, old_one, cur[C : 2 * C, now])
        two = jnp.where(lane >= 2 * WIN, old_two, cur[0:C, now])
        total = act[group, row].astype(F32) + biases[layer] + cur[2 * C : 3 * C, now]
        total = total + pltpu.roll(one, WIN, 1) + pltpu.roll(two, 2 * WIN, 1)
        stored = total.astype(BF16)
        act[group, row] = stored
        if layer + 1 < LAYERS:
            prepare(layer + 1, group, row, stored)

    def emit(layer, group):
        for pair in range(ROWS // 2):
            even = act[group, HALO + 2 * pair]
            odd = pltpu.roll(act[group, HALO + 2 * pair + 1], OWN, 1)
            out[layer, group * 2 + pair] = jnp.where(middle, even, odd)

    def loop(count, step, unroll=1):
        def run(index, _):
            step(index)
            return 0

        lax.fori_loop(0, count, run, 0, unroll=unroll)

    copies = [
        pltpu.make_async_copy(gathered.at[layer], weight.at[layer], arrived.at[layer]) for layer in range(LAYERS)
    ]
    for copy in copies:
        copy.start()
    for at, part in enumerate((f0, f1, f2, f3, f4)):
        act[:, at * ROWS : (at + 1) * ROWS] = part[...]
    for layer in range(LAYERS):
        copies[layer].wait()

        def column(at, layer=layer):
            parts = [weight[layer, 0:C, at + 8 * i : at + 8 * i + 1].astype(F32) for i in range(3)]
            return jnp.broadcast_to(parts[0] + parts[1] + parts[2], (C, 128))

        gains[layer] = 0.5 * column(TAPS)
        biases[layer] = column(TAPS + 1)
    def mixed(one, two):
        return pltpu.roll(jnp.where(lane >= 64, one, two), 64, 1)

    for layer in range(LAYERS):
        source, pairs = spare[layer % 2], HIGH // 2 - layer - 1
        for at in range(2 * pairs + 1):
            low = (layer + at) // 2
            stored = (c0, c1, c2, c3, c4)[low // 2][layer, low % 2]
            if (layer + at) % 2:
                stored = mixed(stored, (c0, c1, c2, c3, c4)[(low + 1) // 2][layer, (low + 1) % 2])
            put(source, at // 2 + at % 2 * ODD, stored)
        parts = [source[:, at * 128 : (at + pairs) * 128] for at in (0, ODD, 1)]
        early[:, STARTS[layer] * 64 : STARTS[layer + 1] * 64] = jnp.dot(
            weight[layer, 0 : 2 * C, 0:TAPS], jnp.concatenate(parts, axis=0), preferred_element_type=F32
        )
    for row in range(HIGH):
        prepare(0, 0, row, act[0, row])

    behind = None
    for layer in range(LAYERS):
        rows = HIGH - 2 * layer - 2
        for group in range(GROUPS):

            multiply(layer, taps[group], layer, rows, 3 * C, sums[group], 0)
            if layer == 0 and group + 1 < GROUPS:
                for row in range(HIGH):
                    prepare(0, group + 1, row, act[group + 1, row])
            if behind is not None:
                for row in range(behind[0] + 1, HIGH - behind[0] - 1):
                    finish(*behind, row)
                emit(*behind)
            behind = (layer, group)
    loop(ROWS, lambda index: finish(*behind, LAYERS + index))
    emit(*behind)


def join_kernel(parts, out):
    lane = lax.broadcasted_iota(jnp.int32, (C, 128), 1)
    for at in range(FRAMES // 2):
        tiles = [shifted(parts[source, at], HALO) for source in range(LAYERS)]
        for bit in (1, 2, 4):
            low = (lane // OWN) % (2 * bit) < bit
            for first in range(LAYERS):
                if first & bit:
                    continue
                one, two = tiles[first], tiles[first + bit]
                tiles[first] = jnp.where(low, one, shifted(two, -OWN * bit))
                tiles[first + bit] = jnp.where(low, shifted(one, OWN * bit), two)
        for k in range(LAYERS):
            out[at // 2 * GROUP + k // 2, at % 2 * 2 + k % 2] = tiles[k]


def along(block, axes, distance):
    count = lax.axis_size(axes)
    route = [(i, i + distance) for i in range(count) if 0 <= i + distance < count]
    return lax.ppermute(block, axes, route)


def mended(place, block, ends, halved=False):
    sections, cols = lax.axis_size("section"), lax.axis_size("col")
    last = (sections - 1) * cols
    route = [(i, i + 1) for i in range(cols - 1)] + [(last + i + 1, last + i) for i in range(cols - 1)]
    beyond = lax.ppermute(ends, ("section", "col"), route)
    tiles = block.reshape(-1, C, 128)
    counts = [tiles.shape[0], tiles.shape[0] // 2][: 1 + halved]
    whole, *first = pl.pallas_call(
        mend_kernel,
        in_specs=[SMEM] + [VMEM] * 2,
        out_shape=[jax.ShapeDtypeStruct((count, C, 128), BF16) for count in counts],
        out_specs=[VMEM] * len(counts),
        compiler_params=vmem(32),
        name="mend",
    )(place, tiles, beyond)
    return whole.reshape(block.shape), *(half.reshape(-1, *block.shape[1:]) for half in first)


def vmem(size):
    return pltpu.CompilerParams(vmem_limit_bytes=size << 20)


def body(features, conv_weight, norm_gain, conv_bias, cached):
    section = lax.axis_index("section")
    row = lax.axis_index(("x", "core"))
    col = lax.axis_index("col")
    place = jnp.stack([section, lax.axis_index("core")]).astype(jnp.int32)

    small = jnp.concatenate([norm_gain, conv_bias, jnp.zeros((6, C), F32)], axis=0)
    mine = pl.pallas_call(
        weights_kernel,
        in_specs=[SMEM] + [VMEM] * 2,
        out_shape=jax.ShapeDtypeStruct((HALF, WIDE), BF16),
        out_specs=VMEM,
        scratch_shapes=[pltpu.VMEM((3 * C, WIDE), BF16)],
        compiler_params=vmem(32),
        name="weights",
    )(place, conv_weight.reshape(3, TAPS, C), small)
    gathered = lax.all_gather(mine, ("section", "core")).reshape(LAYERS, 3 * C, WIDE)

    own, spread, ends = pl.pallas_call(
        windows_kernel,
        in_specs=[SMEM] + [VMEM] * 2,
        out_shape=[
            jax.ShapeDtypeStruct((GROUPS, ROWS, C, 128), BF16),
            jax.ShapeDtypeStruct((LAYERS, 2, C, 128), BF16),
            jax.ShapeDtypeStruct((GROUPS, C, 128), BF16),
        ],
        out_specs=[VMEM] * 3,
        compiler_params=vmem(32),
        name="windows",
    )(place, features, cached[0])
    stored = lax.all_to_all(spread, "section", 0, 0, tiled=True)
    (own,) = mended(place, own, ends)
    steps = (1, -1, 2, -2)
    f = [along(own, ("x", "core"), d) for d in steps]
    stored, *f = lax.optimization_barrier((stored, *f))
    f = [f[2], f[0], own, f[1], f[3]]
    ends = pl.pallas_call(
        ends_kernel,
        in_specs=[SMEM, VMEM],
        out_shape=jax.ShapeDtypeStruct((LAYERS // 2, C, 128), BF16),
        out_specs=VMEM,
        compiler_params=vmem(32),
        name="ends",
    )(place, stored.reshape(2 * LAYERS, C, 128))
    stored, first = mended(place, stored, ends, True)
    c = [along(first if abs(d) == 2 else stored, ("x", "core"), d) for d in steps]
    c = [c[2], c[0], stored, c[1], c[3]]

    at_row = row * ROWS - HALO + jnp.arange(HIGH, dtype=jnp.int32)[:, None, None]
    at_col = col * COLS + section * OWN - HALO + jnp.arange(128, dtype=jnp.int32)[None, None, :] % WIN
    high = lax.axis_size(("x", "core")) * ROWS
    wide = lax.axis_size("col") * COLS
    inside = (at_row >= 0) & (at_row < high) & (at_col >= 0) & (at_col < wide)
    inside = inside.astype(F32)

    packed = pl.pallas_call(
        blocks_kernel,
        in_specs=[VMEM] * 11 + [pl.BlockSpec(memory_space=pl.ANY)],
        out_shape=jax.ShapeDtypeStruct((LAYERS, FRAMES // 2, C, 128), BF16),
        out_specs=VMEM,
        scratch_shapes=[
            pltpu.VMEM((GROUPS, HIGH, C, 128), BF16),
            *[pltpu.VMEM((3 * C, HIGH * 128), BF16)] * GROUPS,
            *[pltpu.VMEM((3 * C, (HIGH - 2) * 128), F32)] * GROUPS,
            pltpu.VMEM((2 * C, STARTS[LAYERS] * 64), F32),
            pltpu.VMEM((LAYERS, C, 128), F32),
            pltpu.VMEM((LAYERS, C, 128), F32),
            pltpu.VMEM((LAYERS, 3 * C, WIDE), BF16),
            *[pltpu.VMEM((3 * C, HIGH * 128), BF16)] * 2,
            pltpu.SemaphoreType.DMA((LAYERS,)),
        ],
        compiler_params=vmem(56),
        cost_estimate=pl.CostEstimate(flops=18_000_000_000, bytes_accessed=8_000_000, transcendentals=0),
        name="blocks",
    )(*f, *c, inside, gathered)
    parts = lax.all_to_all(packed, "section", 0, 0, tiled=True)
    joined = pl.pallas_call(
        join_kernel,
        in_specs=[VMEM],
        out_shape=jax.ShapeDtypeStruct((FRAMES, ROWS, C, COLS), BF16),
        out_specs=VMEM,
        compiler_params=vmem(32),
        name="join",
    )(parts)
    return joined[None]


def solution(mesh):
    sections, rows, cols = (mesh.shape[name] for name in ("section", "row", "col"))
    cores = jax.sharding.Mesh(mesh.devices.reshape(sections, rows // 2, 2, cols), ("section", "x", "core", "col"))
    return jax.shard_map(
        body,
        mesh=cores,
        in_specs=(
            P(None, ("x", "core"), None, "col"),
            P("section", None, None, None, None, None),
            P("section", None),
            P("section", None),
            P("section", None, ("x", "core"), None, "col"),
        ),
        out_specs=P("section", None, ("x", "core"), None, "col"),
        check_vma=False,
    )
```

```python
import jax
import jax.numpy as jnp
from jax import lax
from jax.experimental import pallas as pl
from jax.experimental.pallas import tpu as pltpu
from jax.sharding import PartitionSpec as P

C = 96
LAYERS = 8
FRAMES = 12
ROWS = 4
COLS = 128
OWN = 16
HALO = 8
WIN = OWN + 2 * HALO
GROUPS = 3
GROUP = 4
HIGH = ROWS + 2 * HALO
TAPS = 9 * C
WIDE = 896
VMEM = pl.BlockSpec(memory_space=pltpu.VMEM)
SMEM = pl.BlockSpec(memory_space=pltpu.SMEM)
F32 = jnp.float32
BF16 = jnp.bfloat16


def shifted(block, offset):
    size = block.shape[-1]
    offset %= size
    return pltpu.roll(block, size - offset, 1) if offset else block


def weights_kernel(place, taps, small, out, whole):
    for time in range(3):
        whole[time * C : (time + 1) * C, 0:TAPS] = taps[time].T
    values = small[...].T
    high = values.astype(BF16)
    rest = values - high.astype(F32)
    mid = rest.astype(BF16)
    low = (rest - mid.astype(F32)).astype(BF16)
    whole[0:C, TAPS:WIDE] = jnp.concatenate([high, mid, low, jnp.zeros((C, 8), BF16)], axis=1)
    whole[C : 3 * C, TAPS:WIDE] = jnp.zeros((2 * C, WIDE - TAPS), BF16)
    out[...] = whole[pl.ds(pl.multiple_of(place[1] * HALF, 16), HALF), :]


def gathered_ends(tiles, column):
    lane = lax.broadcasted_iota(jnp.int32, (C, 128), 1)
    total = shifted(tiles[0], column)
    for at in (1, 2, 3):
        total = jnp.where(lane % WIN >= at * HALO, shifted(tiles[at], column - at * HALO), total)
    return total


def windows_kernel(place, features, cached, own, spread, ends):
    lane = lax.broadcasted_iota(jnp.int32, (C, 128), 1)
    section = place[0]

    def joined(pieces):
        total = pieces[0]
        for slot in (1, 2, 3):
            total = jnp.where(lane >= slot * WIN, pieces[slot], total)
        return total

    for target in range(LAYERS):
        for pair in range(ROWS // 2):
            pieces = []
            for slot in range(4):
                tile = cached[slot % 2, 2 * pair + slot // 2]
                pieces.append(shifted(tile, OWN * target - HALO - slot * WIN))
            spread[target, pair] = joined(pieces)
    for group in range(GROUPS):
        for row in range(ROWS):
            pieces = []
            for slot in range(GROUP):
                amount = lax.rem(slot * WIN + HALO - OWN * section + 256, 128)
                pieces.append(pltpu.roll(features[group * GROUP + slot, row], amount, 1))
            own[group, row] = joined(pieces)

    @pl.when(section == 0)
    def _():
        for group in range(GROUPS):
            ends[group] = gathered_ends([own[group, row] for row in range(ROWS)], 0)

    @pl.when(section != 0)
    def _():
        for group in range(GROUPS):
            ends[group] = gathered_ends([own[group, row] for row in range(ROWS)], WIN - HALO)


def ends_kernel(place, block, ends):
    section = place[0]

    @pl.when(section == 0)
    def _():
        for at in range(4):
            ends[at] = gathered_ends([block[at * 4 + i] for i in range(4)], 0)

    @pl.when(section != 0)
    def _():
        for at in range(4):
            ends[at] = gathered_ends([block[at * 4 + i] for i in range(4)], WIN - HALO)


def mend_kernel(place, block, beyond, out, *first):
    lane = lax.broadcasted_iota(jnp.int32, (C, 128), 1) % WIN
    section = place[0]
    out[...] = block[...]

    @pl.when(section == 0)
    def _():
        for at in range(block.shape[0]):
            out[at] = jnp.where(lane < HALO, shifted(beyond[at // 4], at % 4 * HALO), block[at])

    @pl.when(section == LAYERS - 1)
    def _():
        for at in range(block.shape[0]):
            piece = shifted(beyond[at // 4], at % 4 * HALO - (WIN - HALO))
            out[at] = jnp.where(lane >= WIN - HALO, piece, block[at])

    for half in first:
        half[...] = out[0 : half.shape[0]]


ODD = HIGH // 2
STARTS = [sum(HIGH - 2 * i - 2 for i in range(layer)) for layer in range(LAYERS + 1)]
HALF = 3 * C // 2


def blocks_kernel(
    f0, f1, f2, f3, f4, c0, c1, c2, c3, c4, inside, gathered,
    out, act, taps0, taps1, taps2, sums0, sums1, sums2, early, gains, biases, weight, spare0, spare1, arrived,
):
    taps, sums, spare = (taps0, taps1, taps2), (sums0, sums1, sums2), (spare0, spare1)
    lane = lax.broadcasted_iota(jnp.int32, (C, 128), 1)
    middle = jnp.logical_and(lane % WIN >= HALO, lane % WIN < HALO + OWN)

    def tile(row):
        return pl.ds(row * 128 if isinstance(row, int) else pl.multiple_of(row * 128, 128), 128)

    def put(target, row, values):
        target[0:C, tile(row)] = pltpu.roll(values, 1, 1)
        target[C : 2 * C, tile(row)] = values
        target[2 * C : 3 * C, tile(row)] = pltpu.roll(values, 127, 1)

    def prepare(layer, group, row, stored):
        values = stored.astype(F32)
        meansq = jnp.sum(values * values, axis=0, keepdims=True) * (1.0 / C)
        scale = lax.rsqrt(meansq + 1e-06) * inside[row]
        half = values * scale * gains[layer]
        put(taps[group], row, (half * (1.0 + jnp.tanh(half))).astype(BF16))

    def multiply(layer, source, row, count, height, target, column):
        parts = [source[:, pl.ds((row + b) * 128, count * 128)] for b in range(3)]
        target[0:height, pl.ds(column * 128, count * 128)] = jnp.dot(
            weight[layer, 0:height, 0:TAPS], jnp.concatenate(parts, axis=0), preferred_element_type=F32
        )

    def finish(layer, group, row):
        now = tile(row - (layer + 1))
        cur = sums[group]
        if group:
            old_one, old_two = sums[group - 1][C : 2 * C, now], sums[group - 1][0:C, now]
        else:
            pair = tile((row - (layer + 1) + STARTS[layer]) // 2)
            old_one, old_two = early[C : 2 * C, pair], early[0:C, pair]
            if (row - layer) % 2:
                old_one, old_two = pltpu.roll(old_one, 64, 1), pltpu.roll(old_two, 64, 1)
        one = jnp.where(lane >= 3 * WIN, old_one, cur[C : 2 * C, now])
        two = jnp.where(lane >= 2 * WIN, old_two, cur[0:C, now])
        total = act[group, row].astype(F32) + biases[layer] + cur[2 * C : 3 * C, now]
        total = total + pltpu.roll(one, WIN, 1) + pltpu.roll(two, 2 * WIN, 1)
        stored = total.astype(BF16)
        act[group, row] = stored
        if layer + 1 < LAYERS:
            prepare(layer + 1, group, row, stored)

    def emit(layer, group):
        for pair in range(ROWS // 2):
            even = act[group, HALO + 2 * pair]
            odd = pltpu.roll(act[group, HALO + 2 * pair + 1], OWN, 1)
            out[layer, group * 2 + pair] = jnp.where(middle, even, odd)

    def loop(count, step, unroll=1):
        def run(index, _):
            step(index)
            return 0

        lax.fori_loop(0, count, run, 0, unroll=unroll)

    copies = [
        pltpu.make_async_copy(gathered.at[layer], weight.at[layer], arrived.at[layer]) for layer in range(LAYERS)
    ]
    for copy in copies:
        copy.start()
    for at, part in enumerate((f0, f1, f2, f3, f4)):
        act[:, at * ROWS : (at + 1) * ROWS] = part[...]
    for layer in range(LAYERS):
        copies[layer].wait()

        def column(at, layer=layer):
            parts = [weight[layer, 0:C, at + 8 * i : at + 8 * i + 1].astype(F32) for i in range(3)]
            return jnp.broadcast_to(parts[0] + parts[1] + parts[2], (C, 128))

        gains[layer] = 0.5 * column(TAPS)
        biases[layer] = column(TAPS + 1)
    def mixed(one, two):
        return pltpu.roll(jnp.where(lane >= 64, one, two), 64, 1)

    for layer in range(LAYERS):
        source, pairs = spare[layer % 2], HIGH // 2 - layer - 1
        for at in range(2 * pairs + 1):
            low = (layer + at) // 2
            stored = (c0, c1, c2, c3, c4)[low // 2][layer, low % 2]
            if (layer + at) % 2:
                stored = mixed(stored, (c0, c1, c2, c3, c4)[(low + 1) // 2][layer, (low + 1) % 2])
            put(source, at // 2 + at % 2 * ODD, stored)
        parts = [source[:, at * 128 : (at + pairs) * 128] for at in (0, ODD, 1)]
        early[:, STARTS[layer] * 64 : STARTS[layer + 1] * 64] = jnp.dot(
            weight[layer, 0 : 2 * C, 0:TAPS], jnp.concatenate(parts, axis=0), preferred_element_type=F32
        )
    for row in range(HIGH):
        prepare(0, 0, row, act[0, row])

    behind = None
    for layer in range(LAYERS):
        rows = HIGH - 2 * layer - 2
        for group in range(GROUPS):

            multiply(layer, taps[group], layer, rows, 3 * C, sums[group], 0)
            if layer == 0 and group + 1 < GROUPS:
                for row in range(HIGH):
                    prepare(0, group + 1, row, act[group + 1, row])
            if behind is not None:
                for row in range(behind[0] + 1, HIGH - behind[0] - 1):
                    finish(*behind, row)
                emit(*behind)
            behind = (layer, group)
    loop(ROWS, lambda index: finish(*behind, LAYERS + index))
    emit(*behind)


def join_kernel(parts, out):
    lane = lax.broadcasted_iota(jnp.int32, (C, 128), 1)
    for at in range(FRAMES // 2):
        tiles = [shifted(parts[source, at], HALO) for source in range(LAYERS)]
        for bit in (1, 2, 4):
            low = (lane // OWN) % (2 * bit) < bit
            for first in range(LAYERS):
                if first & bit:
                    continue
                one, two = tiles[first], tiles[first + bit]
                tiles[first] = jnp.where(low, one, shifted(two, -OWN * bit))
                tiles[first + bit] = jnp.where(low, shifted(one, OWN * bit), two)
        for k in range(LAYERS):
            out[at // 2 * GROUP + k // 2, at % 2 * 2 + k % 2] = tiles[k]


def along(block, axes, distance):
    count = lax.axis_size(axes)
    route = [(i, i + distance) for i in range(count) if 0 <= i + distance < count]
    return lax.ppermute(block, axes, route)


def mended(place, block, ends, halved=False):
    sections, cols = lax.axis_size("section"), lax.axis_size("col")
    last = (sections - 1) * cols
    route = [(i, i + 1) for i in range(cols - 1)] + [(last + i + 1, last + i) for i in range(cols - 1)]
    beyond = lax.ppermute(ends, ("section", "col"), route)
    tiles = block.reshape(-1, C, 128)
    counts = [tiles.shape[0], tiles.shape[0] // 2][: 1 + halved]
    whole, *first = pl.pallas_call(
        mend_kernel,
        in_specs=[SMEM] + [VMEM] * 2,
        out_shape=[jax.ShapeDtypeStruct((count, C, 128), BF16) for count in counts],
        out_specs=[VMEM] * len(counts),
        compiler_params=vmem(32),
        name="mend",
    )(place, tiles, beyond)
    return whole.reshape(block.shape), *(half.reshape(-1, *block.shape[1:]) for half in first)


def vmem(size):
    return pltpu.CompilerParams(vmem_limit_bytes=size << 20)


def body(features, conv_weight, norm_gain, conv_bias, cached):
    section = lax.axis_index("section")
    row = lax.axis_index(("x", "core"))
    col = lax.axis_index("col")
    place = jnp.stack([section, lax.axis_index("core")]).astype(jnp.int32)

    small = jnp.concatenate([norm_gain, conv_bias, jnp.zeros((6, C), F32)], axis=0)
    mine = pl.pallas_call(
        weights_kernel,
        in_specs=[SMEM] + [VMEM] * 2,
        out_shape=jax.ShapeDtypeStruct((HALF, WIDE), BF16),
        out_specs=VMEM,
        scratch_shapes=[pltpu.VMEM((3 * C, WIDE), BF16)],
        compiler_params=vmem(32),
        name="weights",
    )(place, conv_weight.reshape(3, TAPS, C), small)
    gathered = lax.all_gather(mine, ("section", "core")).reshape(LAYERS, 3 * C, WIDE)

    own, spread, ends = pl.pallas_call(
        windows_kernel,
        in_specs=[SMEM] + [VMEM] * 2,
        out_shape=[
            jax.ShapeDtypeStruct((GROUPS, ROWS, C, 128), BF16),
            jax.ShapeDtypeStruct((LAYERS, 2, C, 128), BF16),
            jax.ShapeDtypeStruct((GROUPS, C, 128), BF16),
        ],
        out_specs=[VMEM] * 3,
        compiler_params=vmem(32),
        name="windows",
    )(place, features, cached[0])
    stored = lax.all_to_all(spread, "section", 0, 0, tiled=True)
    (own,) = mended(place, own, ends)
    steps = (1, -1, 2, -2)
    f = [along(own, ("x", "core"), d) for d in steps]
    stored, *near = lax.optimization_barrier((stored, *f[:2]))
    f = [f[2], near[0], own, near[1], f[3]]
    ends = pl.pallas_call(
        ends_kernel,
        in_specs=[SMEM, VMEM],
        out_shape=jax.ShapeDtypeStruct((LAYERS // 2, C, 128), BF16),
        out_specs=VMEM,
        compiler_params=vmem(32),
        name="ends",
    )(place, stored.reshape(2 * LAYERS, C, 128))
    stored, first = mended(place, stored, ends, True)
    c = [along(first if abs(d) == 2 else stored, ("x", "core"), d) for d in steps]
    c = [c[2], c[0], stored, c[1], c[3]]

    at_row = row * ROWS - HALO + jnp.arange(HIGH, dtype=jnp.int32)[:, None, None]
    at_col = col * COLS + section * OWN - HALO + jnp.arange(128, dtype=jnp.int32)[None, None, :] % WIN
    high = lax.axis_size(("x", "core")) * ROWS
    wide = lax.axis_size("col") * COLS
    inside = (at_row >= 0) & (at_row < high) & (at_col >= 0) & (at_col < wide)
    inside = inside.astype(F32)

    packed = pl.pallas_call(
        blocks_kernel,
        in_specs=[VMEM] * 11 + [pl.BlockSpec(memory_space=pl.ANY)],
        out_shape=jax.ShapeDtypeStruct((LAYERS, FRAMES // 2, C, 128), BF16),
        out_specs=VMEM,
        scratch_shapes=[
            pltpu.VMEM((GROUPS, HIGH, C, 128), BF16),
            *[pltpu.VMEM((3 * C, HIGH * 128), BF16)] * GROUPS,
            *[pltpu.VMEM((3 * C, (HIGH - 2) * 128), F32)] * GROUPS,
            pltpu.VMEM((2 * C, STARTS[LAYERS] * 64), F32),
            pltpu.VMEM((LAYERS, C, 128), F32),
            pltpu.VMEM((LAYERS, C, 128), F32),
            pltpu.VMEM((LAYERS, 3 * C, WIDE), BF16),
            *[pltpu.VMEM((3 * C, HIGH * 128), BF16)] * 2,
            pltpu.SemaphoreType.DMA((LAYERS,)),
        ],
        compiler_params=vmem(56),
        cost_estimate=pl.CostEstimate(flops=18_000_000_000, bytes_accessed=8_000_000, transcendentals=0),
        name="blocks",
    )(*f, *c, inside, gathered)
    parts = lax.all_to_all(packed, "section", 0, 0, tiled=True)
    joined = pl.pallas_call(
        join_kernel,
        in_specs=[VMEM],
        out_shape=jax.ShapeDtypeStruct((FRAMES, ROWS, C, COLS), BF16),
        out_specs=VMEM,
        compiler_params=vmem(32),
        name="join",
    )(parts)
    return joined[None]


def solution(mesh):
    sections, rows, cols = (mesh.shape[name] for name in ("section", "row", "col"))
    cores = jax.sharding.Mesh(mesh.devices.reshape(sections, rows // 2, 2, cols), ("section", "x", "core", "col"))
    return jax.shard_map(
        body,
        mesh=cores,
        in_specs=(
            P(None, ("x", "core"), None, "col"),
            P("section", None, None, None, None, None),
            P("section", None),
            P("section", None),
            P("section", None, ("x", "core"), None, "col"),
        ),
        out_specs=P("section", None, ("x", "core"), None, "col"),
        check_vma=False,
    )
```
